128 devices in a mesh: dp: 8 (over z, x_lo), seq: 16 (over x_hi, y, core).
Axes of the slice: x: 4 (x_hi: 2, x_lo: 2; x = x_hi * 2 + x_lo), y: 4, z: 4, core: 2. Of those that a mesh axis runs over, the one named last changes fastest.
Arguments:
- tokens: bfloat16 [8, 16384, 2048], P('dp', 'seq'), may hold values from -6 to 6
- gate: bfloat16 [8, 16384, 2048], P('dp', 'seq'), may hold values from -6 to 6
- cotangent: bfloat16 [8, 16384, 2048], P('dp', 'seq'), may hold values from -6 to 6
- first_factor: bfloat16 [32, 512, 512], P('seq'), may hold values from -0.25 to 0.25
- second_factor: bfloat16 [512, 32, 32], P('seq'), may hold values from -1 to 1
Outputs:
- input_grad: bfloat16 [8, 16384, 2048], P('dp', 'seq')
- gate_grad: bfloat16 [8, 16384, 2048], P('dp', 'seq')
- first_grad: float32 [32, 512, 512], P('seq', 'dp')
- second_grad: float32 [512, 32, 32], P('seq', 'dp')
The draws below stay inside these ranges and needn't reach their ends.
All inputs are finite; a program needn't handle non-finite values.
Results may differ from the reference program's by a relative error of at most 0.0057.
Values may be sent and summed in bfloat16 or wider, within the bound.
A program may use at most 128 MiB of HBM per device.

```python
import jax
import jax.numpy as jnp
from jax import lax

D = 2048
BS = 512
NB = 32
SEQ_LEN = 16384
BATCH = 8


def block_levels(own_key, dims, split, least, high):
    factor_of, own = 1.0, jax.random.fold_in(own_key, 6)
    for dim, blocks in split:
        steps = jnp.exp(jax.random.uniform(jax.random.fold_in(own, dim), (blocks,), jnp.float32, least / len(split), high / len(split)))
        factor_of = factor_of * jnp.repeat(steps, dims[dim] // blocks).reshape([-1 if axis == dim else 1 for axis in range(len(dims))])
    return factor_of


def normal_values(stream_key, dims, spread, reach, pieces=(), kind=jnp.bfloat16):
    entries = spread * jax.random.normal(stream_key, dims, jnp.float32)
    if pieces:
        entries = entries * block_levels(stream_key, dims, pieces, -0.22, 0.18)
    return jnp.clip(entries, -reach, reach).astype(kind)


def setup_inputs(seed: int = 0) -> dict:
    arg_keys = jax.random.split(jax.random.key(seed), 6)
    tokens = normal_values(arg_keys[0], (BATCH, SEQ_LEN, D), 1.0, 6.0, ((0, 8), (1, 16)))
    gate = normal_values(arg_keys[1], (BATCH, SEQ_LEN, D), 1.0, 6.0, ((0, 8), (1, 16)))
    cotangent = normal_values(arg_keys[2], (BATCH, SEQ_LEN, D), 1.0, 6.0, ((0, 8), (1, 16)))
    first_factor = normal_values(arg_keys[3], (NB, BS, BS), BS ** -0.5, 0.25, ((0, 16),))
    second_factor = normal_values(arg_keys[4], (BS, NB, NB), NB ** -0.5, 1.0, ((0, 16),))
    return dict(tokens=tokens, gate=gate, cotangent=cotangent, first_factor=first_factor, second_factor=second_factor)


def reference(tokens, gate, cotangent, first_factor, second_factor):
    first_wide = first_factor.astype(jnp.float32)
    second_wide = second_factor.astype(jnp.float32)
    highest = lax.Precision.HIGHEST

    def one_sequence(carry, inputs):
        first_acc, second_acc = carry
        seq_in, seq_gate, seq_cot = inputs
        blocks = seq_in.reshape(NB, BS, D).astype(jnp.float32)
        hidden = jnp.einsum('bij,bjc->bic', first_wide, blocks, precision=highest).astype(jnp.bfloat16)
        hidden_wide = hidden.astype(jnp.float32)
        mixed = jnp.einsum('ipb,bic->ipc', second_wide, hidden_wide, precision=highest)
        gate_t = seq_gate.reshape(BS, NB, D).astype(jnp.float32)
        cot_t = seq_cot.reshape(BS, NB, D).astype(jnp.float32)
        gate_grad = (cot_t * mixed).astype(jnp.bfloat16).reshape(SEQ_LEN, D)
        mixed_grad = (cot_t * gate_t).astype(jnp.bfloat16).astype(jnp.float32)
        second_acc = second_acc + jnp.einsum('ipc,bic->ipb', mixed_grad, hidden_wide, precision=highest)
        hidden_grad = jnp.einsum('ipb,ipc->bic', second_wide, mixed_grad, precision=highest).astype(jnp.bfloat16)
        hidden_grad_wide = hidden_grad.astype(jnp.float32)
        first_acc = first_acc + jnp.einsum('bic,bjc->bij', hidden_grad_wide, blocks, precision=highest)
        input_grad = jnp.einsum('bij,bic->bjc', first_wide, hidden_grad_wide, precision=highest)
        input_grad = input_grad.astype(jnp.bfloat16).reshape(SEQ_LEN, D)
        return ((first_acc, second_acc), (input_grad, gate_grad))
    start = (jnp.zeros((NB, BS, BS), jnp.float32), jnp.zeros((BS, NB, NB), jnp.float32))
    (first_acc, second_acc), (input_grad, gate_grad) = lax.scan(one_sequence, start, (tokens, gate, cotangent))
    factor = 1.0 / jnp.sqrt(jnp.float32(D * BATCH))
    return (input_grad, gate_grad, first_acc * factor, second_acc * factor)
```

```python
import functools
import math

import jax
import jax.numpy as jnp
from jax import lax
from jax.experimental import pallas as pl
from jax.experimental.pallas import tpu as pltpu
from jax.sharding import PartitionSpec as P

MESH = pl.DeviceIdType.MESH
F32, BF16 = jnp.float32, jnp.bfloat16
CHUNKS = 8
SEQ, DP = 16, 8
NB, BS, G = 32, 512, 16
NT = (((1,), (1,)), ((), ()))


def iota(shape, dim):
    return lax.broadcasted_iota(jnp.int32, shape, dim)


def kernel(
    width, scale,
    tok, gate, cot, first, second,
    ig, gg, fo, so,
    tok_v, cot_v, mg_v, f_v, ft_v, s_v, w_v, wt_v,
    hg_send, h_send, hg_recv, h_recv,
    facc, sacc, zrecv, xsend, xrecv, xkeep, sec_send, sec_recv,
    load_sem, fac_sem, hg_ss, hg_rs, h_ss, h_rs, z_ss, z_rs, x_ss, x_rs, s_ss, s_rs,
):
    cw = width // CHUNKS
    dp, me = lax.axis_index("dp"), lax.axis_index("seq")
    z, xl = dp // 2, dp % 2

    def chunk_loads(k):
        cols = pl.ds(pl.multiple_of(k * cw, cw), cw)
        return (
            pltpu.make_async_copy(cot.at[:, cols], cot_v.at[k], load_sem.at[0, k]),
            pltpu.make_async_copy(gate.at[:, cols], mg_v.at[k], load_sem.at[1, k]),
            pltpu.make_async_copy(tok.at[:, cols], tok_v.at[k], load_sem.at[2, k]),
        )

    load_second = pltpu.make_async_copy(second, s_v, fac_sem.at[0])
    load_first = pltpu.make_async_copy(first, f_v, fac_sem.at[1])
    load_second.start()

    def start_pair(k, carry):
        a, b, _ = chunk_loads(k)
        a.start()
        b.start()
        return carry

    def start_tok(k, carry):
        chunk_loads(k)[2].start()
        return carry

    lax.fori_loop(0, CHUNKS, start_pair, 0)
    load_first.start()
    lax.fori_loop(0, CHUNKS, start_tok, 0)

    barrier = pltpu.get_barrier_semaphore()

    def greet_seq(p, carry):
        pl.semaphore_signal(barrier, inc=1, device_id=(dp, (me + p) % SEQ), device_id_type=MESH)
        return carry

    def greet_dp(p, carry):
        pl.semaphore_signal(barrier, inc=1, device_id=((dp + p) % DP, me), device_id_type=MESH)
        return carry

    lax.fori_loop(1, SEQ, greet_seq, 0)
    lax.fori_loop(1, DP, greet_dp, 0)

    load_second.wait()
    n = G * NB
    spread = (iota((n, NB), 0) // G == iota((n, NB), 1)).astype(BF16)
    same = iota((n, n), 0) // NB == iota((n, n), 1) % G
    same_t = iota((n, n), 1) // NB == iota((n, n), 0) % G
    for g in range(2):
        s_g = s_v[g * n : (g + 1) * n, :]
        w = lax.dot_general(s_g, spread, NT, preferred_element_type=F32)
        w_v[g] = jnp.where(same, w, 0.0).astype(BF16)
        wt = lax.dot_general(spread, s_g, NT, preferred_element_type=F32)
        wt_v[g] = jnp.where(same_t, wt, 0.0).astype(BF16)

    def send(src, dst, k, ss, rs):
        place = dst.at[k, :, pl.ds(2 * me, 2)]

        def one(p, carry):
            t = (me + p) % SEQ
            pltpu.make_async_remote_copy(
                src_ref=src.at[k, t], dst_ref=place, send_sem=ss.at[k], recv_sem=rs.at[k],
                device_id=(dp, t), device_id_type=MESH,
            ).start()
            return carry

        lax.fori_loop(1, SEQ, one, 0)
        pltpu.make_async_copy(src.at[k, me], place, rs.at[k]).start()

    def wait_sent(src, k, ss):
        ref = src.at[k, pl.ds(0, SEQ - 1)]
        pltpu.make_async_copy(ref, ref, ss.at[k]).wait()

    def wait_all(dst, k, rs):
        pltpu.make_async_copy(dst.at[k], dst.at[k], rs.at[k]).wait()

    def make_hg(k):
        a, b, _ = chunk_loads(k)
        a.wait()
        b.wait()
        for g in range(2):
            rows = slice(g * n, (g + 1) * n)
            m = (cot_v[k, rows, :].astype(F32) * mg_v[k, rows, :].astype(F32)).astype(BF16)
            mg_v[k, rows, :] = m
            hg = jnp.dot(wt_v[g], m, preferred_element_type=F32).astype(BF16)
            hg_send[k, :, :, g] = hg.reshape(SEQ, 2, G, cw)

    make_hg(0)
    pl.semaphore_wait(barrier, SEQ - 1 + DP - 1)
    send(hg_send, hg_recv, 0, hg_ss, hg_rs)

    def hg_step(k, carry):
        make_hg(k)
        send(hg_send, hg_recv, k, hg_ss, hg_rs)
        return carry

    lax.fori_loop(1, CHUNKS, hg_step, 0)

    load_first.wait()

    def h_step(k, carry):
        chunk_loads(k)[2].wait()
        for b in range(2):
            h = jnp.dot(f_v[b], tok_v[k, b * BS : (b + 1) * BS, :], preferred_element_type=F32)
            h_send[k, :, :, b] = h.astype(BF16).reshape(SEQ, 2, G, cw)
        return carry

    lax.fori_loop(0, CHUNKS, h_step, 0)
    for b in range(2):
        ft_v[b] = f_v[b].T

    facc[...] = jnp.zeros_like(facc)
    sacc[...] = jnp.zeros_like(sacc)

    def back_step(k, carry):
        wait_sent(hg_send, k, hg_ss)
        send(h_send, h_recv, k, h_ss, h_rs)
        wait_all(hg_recv, k, hg_rs)
        cols = pl.ds(pl.multiple_of(k * cw, cw), cw)
        for b in range(2):
            hg = hg_recv[k, b].reshape(BS, cw)
            rows = slice(b * BS, (b + 1) * BS)
            ig[rows, cols] = jnp.dot(ft_v[b], hg, preferred_element_type=F32).astype(BF16)
            terms = lax.dot_general(hg, tok_v[k, rows, :], NT, preferred_element_type=F32)
            facc[b] += terms.reshape(4, 2, 64, BS)
        return carry

    lax.fori_loop(0, CHUNKS, back_step, 0)

    def z_copy(d):
        t = (z + d) % 4
        return pltpu.make_async_remote_copy(
            src_ref=facc.at[:, t], dst_ref=zrecv.at[d - 1],
            send_sem=z_ss.at[d - 1], recv_sem=z_rs.at[d - 1],
            device_id=(t * 2 + xl, me), device_id_type=MESH,
        )

    x_copy = pltpu.make_async_remote_copy(
        src_ref=xsend, dst_ref=xrecv, send_sem=x_ss, recv_sem=x_rs,
        device_id=(z * 2 + 1 - xl, me), device_id_type=MESH,
    )
    for d in (1, 2, 3):
        z_copy(d).start()

    def forth_step(k, carry):
        wait_all(h_recv, k, h_rs)
        cols = pl.ds(pl.multiple_of(k * cw, cw), cw)
        for g in range(2):
            h = h_recv[k, g].reshape(n, cw)
            rows = slice(g * n, (g + 1) * n)
            mixed = jnp.dot(w_v[g], h, preferred_element_type=F32)
            gg[rows, cols] = (cot_v[k, rows, :].astype(F32) * mixed).astype(BF16)
            sacc[g] += lax.dot_general(mg_v[k, rows, :], h, NT, preferred_element_type=F32)
        return carry

    half = CHUNKS // 2
    lax.fori_loop(0, half, forth_step, 0)

    for d in (1, 2, 3):
        z_copy(d).wait()
    for b in range(2):
        other = facc[b, z, 1 - xl] + zrecv[0, b, 1 - xl] + zrecv[1, b, 1 - xl] + zrecv[2, b, 1 - xl]
        xsend[b] = other.astype(BF16)
    x_copy.start()
    for b in range(2):
        xkeep[b] = facc[b, z, xl] + zrecv[0, b, xl] + zrecv[1, b, xl] + zrecv[2, b, xl]

    lax.fori_loop(half, CHUNKS - 1, forth_step, 0)
    x_copy.wait()
    fo[...] = (xkeep[...] + xrecv[...].astype(F32)) * scale
    forth_step(CHUNKS - 1, 0)

    high = lax.Precision.HIGHEST
    gather = (iota((n, 128), 0) // G == iota((n, 128), 1) % NB).astype(F32)
    inner = iota((n, 128), 0) % 4 == iota((n, 128), 1) // NB
    at, of = iota((128, n), 0), iota((128, n), 1)
    pick = ((at % G == of // NB) & (at // G == of % NB // 4)).astype(F32)
    for g in range(2):
        own = jnp.where(same, sacc[g], 0.0)
        wide = jnp.dot(own, gather, precision=high, preferred_element_type=F32)
        wide = jnp.where(inner, wide, 0.0)
        share = jnp.dot(pick, wide, precision=high, preferred_element_type=F32)
        sec_send[:, g] = share.reshape(DP, G, 128)

    def s_copy(p):
        t = (dp + p) % DP
        return pltpu.make_async_remote_copy(
            src_ref=sec_send.at[t], dst_ref=sec_recv.at[p - 1],
            send_sem=s_ss.at[p - 1], recv_sem=s_rs.at[p - 1],
            device_id=(t, me), device_id_type=MESH,
        )

    for p in range(1, DP):
        s_copy(p).start()

    def drain(k, carry):
        wait_sent(h_send, k, h_ss)
        return carry

    lax.fori_loop(0, CHUNKS, drain, 0)
    total = sec_send[dp]
    for p in range(1, DP):
        s_copy(p).wait()
        total = total + sec_recv[p - 1]
    so[...] = total * scale


def local(tokens, gate, cotangent, first_factor, second_factor):
    seqs, rows, width = tokens.shape
    scale = 1.0 / math.sqrt(width * seqs * DP)
    cw = width // CHUNKS
    flat = (rows, width)
    vm = pltpu.VMEM
    dma = pltpu.SemaphoreType.DMA
    out = (
        vm(flat, BF16), vm(flat, BF16), vm((2, 64, BS), F32), vm((2, G, 128), F32),
    )
    scratch = [
        vm((CHUNKS, rows, cw), BF16), vm((CHUNKS, rows, cw), BF16), vm((CHUNKS, rows, cw), BF16),
        vm((2, BS, BS), BF16), vm((2, BS, BS), BF16), vm((BS * 2, NB), BF16),
        vm((2, BS, BS), BF16), vm((2, BS, BS), BF16),
        vm((CHUNKS, SEQ, 2, 2, G, cw), BF16), vm((CHUNKS, SEQ, 2, 2, G, cw), BF16),
        vm((CHUNKS, 2, NB, G, cw), BF16), vm((CHUNKS, 2, NB, G, cw), BF16),
        vm((2, 4, 2, 64, BS), F32), vm((2, BS, BS), F32), vm((3, 2, 2, 64, BS), F32),
        vm((2, 64, BS), BF16), vm((2, 64, BS), BF16), vm((2, 64, BS), F32),
        vm((DP, 2, G, 128), F32), vm((DP - 1, 2, G, 128), F32),
        dma((3, CHUNKS)), dma((2,)),
        dma((CHUNKS,)), dma((CHUNKS,)), dma((CHUNKS,)), dma((CHUNKS,)),
        dma((3,)), dma((3,)), dma, dma, dma((DP - 1,)), dma((DP - 1,)),
    ]
    hbm = pl.BlockSpec(memory_space=pl.ANY)
    inner = pl.BlockSpec(memory_space=pltpu.VMEM)
    ig, gg, fo, so = pl.pallas_call(
        functools.partial(kernel, width, scale),
        out_shape=out,
        in_specs=[hbm] * 5,
        out_specs=[inner] * 4,
        scratch_shapes=scratch,
        compiler_params=pltpu.CompilerParams(
            collective_id=0, has_side_effects=True, vmem_limit_bytes=52 * 2**20
        ),
        cost_estimate=pl.CostEstimate(
            flops=15 * 2**30, bytes_accessed=22 * 2**20, transcendentals=0
        ),
        name="mixer",
    )(
        tokens.reshape(flat), gate.reshape(flat), cotangent.reshape(flat),
        first_factor, second_factor.reshape(BS * 2, NB),
    )
    return (
        ig.reshape(seqs, rows, width), gg.reshape(seqs, rows, width),
        fo, so.reshape(NB, 4, NB),
    )


def solution(mesh):
    placed = (
        P("dp", "seq", None),
        P("dp", "seq", None),
        P("dp", "seq", None),
        P("seq", None, None),
        P("seq", None, None),
    )
    return jax.shard_map(
        local,
        mesh=mesh,
        in_specs=placed,
        out_specs=(
            P("dp", "seq", None),
            P("dp", "seq", None),
            P("seq", "dp", None),
            P("seq", "dp", None),
        ),
        check_vma=False,
    )
```

```python
import functools
import math

import jax
import jax.numpy as jnp
from jax import lax
from jax.experimental import pallas as pl
from jax.experimental.pallas import tpu as pltpu
from jax.sharding import PartitionSpec as P

MESH = pl.DeviceIdType.MESH
F32, BF16 = jnp.float32, jnp.bfloat16
CHUNKS = 8
SEQ, DP = 16, 8
NB, BS, G = 32, 512, 16
NT = (((1,), (1,)), ((), ()))


def iota(shape, dim):
    return lax.broadcasted_iota(jnp.int32, shape, dim)


def kernel(
    width, scale,
    tok, gate, cot, first, second,
    ig, gg, fo, so,
    tok_v, cot_v, mg_v, f_v, ft_v, s_v, w_v, wt_v,
    hg_send, h_send, hg_recv, h_recv,
    facc, sacc, zrecv, xsend, xrecv, xkeep, sec_send, sec_recv,
    load_sem, fac_sem, hg_ss, hg_rs, h_ss, h_rs, z_ss, z_rs, x_ss, x_rs, s_ss, s_rs,
):
    cw = width // CHUNKS
    dp, me = lax.axis_index("dp"), lax.axis_index("seq")
    z, xl = dp // 2, dp % 2

    def chunk_loads(k):
        cols = pl.ds(pl.multiple_of(k * cw, cw), cw)
        return (
            (cot.at[:, cols], cot_v.at[k], load_sem.at[0, k]),
            (gate.at[:, cols], mg_v.at[k], load_sem.at[1, k]),
            (tok.at[:, cols], tok_v.at[k], load_sem.at[2, k]),
        )

    def start_loads(k, which):
        for a in which:
            pltpu.make_async_copy(*chunk_loads(k)[a]).start()

    def wait_loads(k, which):
        for a in which:
            pltpu.make_async_copy(*chunk_loads(k)[a]).wait()

    load_second = pltpu.make_async_copy(second, s_v, fac_sem.at[0])
    load_first = pltpu.make_async_copy(first, f_v, fac_sem.at[1])
    load_second.start()
    start_loads(0, (0, 1))

    barrier = pltpu.get_barrier_semaphore()

    def greet_seq(p, carry):
        pl.semaphore_signal(barrier, inc=1, device_id=(dp, (me + p) % SEQ), device_id_type=MESH)
        return carry

    def greet_dp(p, carry):
        pl.semaphore_signal(barrier, inc=1, device_id=((dp + p) % DP, me), device_id_type=MESH)
        return carry

    lax.fori_loop(1, SEQ, greet_seq, 0)
    lax.fori_loop(1, DP, greet_dp, 0)
    start_loads(1, (0, 1))

    load_second.wait()
    n = G * NB
    spread = (iota((n, NB), 0) // G == iota((n, NB), 1)).astype(BF16)
    same = iota((n, n), 0) // NB == iota((n, n), 1) % G
    same_t = iota((n, n), 1) // NB == iota((n, n), 0) % G
    for g in range(2):
        wt = lax.dot_general(
            spread, s_v[g * n : (g + 1) * n, :], NT, preferred_element_type=F32
        )
        wt_v[g] = jnp.where(same_t, wt, 0.0).astype(BF16)

    def send(src, dst, k, ss, rs):
        place = dst.at[k, :, pl.ds(2 * me, 2)]

        def one(p, carry):
            t = (me + p) % SEQ
            pltpu.make_async_remote_copy(
                src_ref=src.at[k, t], dst_ref=place, send_sem=ss.at[k], recv_sem=rs.at[k],
                device_id=(dp, t), device_id_type=MESH,
            ).start()
            return carry

        lax.fori_loop(1, SEQ, one, 0)
        pltpu.make_async_copy(src.at[k, me], place, rs.at[k]).start()

    def wait_sent(src, k, ss):
        ref = src.at[k, pl.ds(0, SEQ - 1)]
        pltpu.make_async_copy(ref, ref, ss.at[k]).wait()

    def wait_all(dst, k, rs):
        pltpu.make_async_copy(dst.at[k], dst.at[k], rs.at[k]).wait()

    def make_hg(k):
        wait_loads(k, (0, 1))
        for g in range(2):
            rows = slice(g * n, (g + 1) * n)
            m = (cot_v[k, rows, :].astype(F32) * mg_v[k, rows, :].astype(F32)).astype(BF16)
            mg_v[k, rows, :] = m
            hg = jnp.dot(wt_v[g], m, preferred_element_type=F32).astype(BF16)
            hg_send[k, :, :, g] = hg.reshape(SEQ, 2, G, cw)

    make_hg(0)
    pl.semaphore_wait(barrier, SEQ - 1 + DP - 1)
    send(hg_send, hg_recv, 0, hg_ss, hg_rs)

    def hg_step(k, carry):
        @pl.when(k < CHUNKS - 1)
        def _():
            start_loads(k + 1, (0, 1))

        make_hg(k)
        send(hg_send, hg_recv, k, hg_ss, hg_rs)
        return carry

    lax.fori_loop(1, CHUNKS, hg_step, 0)

    load_first.start()

    def load_tok(k, carry):
        start_loads(k, (2,))
        return carry

    lax.fori_loop(0, CHUNKS, load_tok, 0)
    for g in range(2):
        w = lax.dot_general(
            s_v[g * n : (g + 1) * n, :], spread, NT, preferred_element_type=F32
        )
        w_v[g] = jnp.where(same, w, 0.0).astype(BF16)
    load_first.wait()

    def h_step(k, carry):
        wait_loads(k, (2,))
        for b in range(2):
            h = jnp.dot(f_v[b], tok_v[k, b * BS : (b + 1) * BS, :], preferred_element_type=F32)
            h_send[k, :, :, b] = h.astype(BF16).reshape(SEQ, 2, G, cw)
        return carry

    lax.fori_loop(0, CHUNKS, h_step, 0)
    for b in range(2):
        ft_v[b] = f_v[b].T

    facc[...] = jnp.zeros_like(facc)
    sacc[...] = jnp.zeros_like(sacc)

    def back_step(k, carry):
        wait_sent(hg_send, k, hg_ss)
        send(h_send, h_recv, k, h_ss, h_rs)
        wait_all(hg_recv, k, hg_rs)
        cols = pl.ds(pl.multiple_of(k * cw, cw), cw)
        for b in range(2):
            hg = hg_recv[k, b].reshape(BS, cw)
            rows = slice(b * BS, (b + 1) * BS)
            ig[rows, cols] = jnp.dot(ft_v[b], hg, preferred_element_type=F32).astype(BF16)
            terms = lax.dot_general(hg, tok_v[k, rows, :], NT, preferred_element_type=F32)
            facc[b] += terms.reshape(4, 2, 64, BS)
        return carry

    lax.fori_loop(0, CHUNKS, back_step, 0)

    def z_copy(d):
        t = (z + d) % 4
        return pltpu.make_async_remote_copy(
            src_ref=facc.at[:, t], dst_ref=zrecv.at[d - 1],
            send_sem=z_ss.at[d - 1], recv_sem=z_rs.at[d - 1],
            device_id=(t * 2 + xl, me), device_id_type=MESH,
        )

    x_copy = pltpu.make_async_remote_copy(
        src_ref=xsend, dst_ref=xrecv, send_sem=x_ss, recv_sem=x_rs,
        device_id=(z * 2 + 1 - xl, me), device_id_type=MESH,
    )
    for d in (1, 2, 3):
        z_copy(d).start()

    def second_terms(k):
        for g in range(2):
            h = h_recv[k, g].reshape(n, cw)
            m = mg_v[k, g * n : (g + 1) * n, :]
            terms = lax.dot_general(m, h, NT, preferred_element_type=F32)
            terms = jnp.where(same, terms, 0.0).reshape(G, NB, n)
            sacc[g] += jnp.sum(terms, axis=0)

    def gate_part(k):
        cols = pl.ds(pl.multiple_of(k * cw, cw), cw)
        for g in range(2):
            h = h_recv[k, g].reshape(n, cw)
            rows = slice(g * n, (g + 1) * n)
            mixed = jnp.dot(w_v[g], h, preferred_element_type=F32)
            gg[rows, cols] = (cot_v[k, rows, :].astype(F32) * mixed).astype(BF16)

    def forth_step(k, carry):
        wait_all(h_recv, k, h_rs)
        second_terms(k)
        gate_part(k)
        return carry

    half = CHUNKS // 2
    lax.fori_loop(0, half, forth_step, 0)

    for d in (1, 2, 3):
        z_copy(d).wait()
    for b in range(2):
        other = facc[b, z, 1 - xl] + zrecv[0, b, 1 - xl] + zrecv[1, b, 1 - xl] + zrecv[2, b, 1 - xl]
        xsend[b] = other.astype(BF16)
    x_copy.start()
    for b in range(2):
        xkeep[b] = facc[b, z, xl] + zrecv[0, b, xl] + zrecv[1, b, xl] + zrecv[2, b, xl]

    lax.fori_loop(half, CHUNKS - 1, forth_step, 0)
    x_copy.wait()
    fo[...] = (xkeep[...] + xrecv[...].astype(F32)) * scale
    wait_all(h_recv, CHUNKS - 1, h_rs)
    second_terms(CHUNKS - 1)
    for g in range(2):
        for d in range(DP):
            sec_send[d, 4 * g : 4 * g + 4] = sacc[g, 4 * d : 4 * d + 4]

    def s_copy(p):
        t = (dp + p) % DP
        return pltpu.make_async_remote_copy(
            src_ref=sec_send.at[t], dst_ref=sec_recv.at[p - 1],
            send_sem=s_ss.at[p - 1], recv_sem=s_rs.at[p - 1],
            device_id=(t, me), device_id_type=MESH,
        )

    for p in range(1, DP):
        s_copy(p).start()
    gate_part(CHUNKS - 1)

    def drain(k, carry):
        wait_sent(h_send, k, h_ss)
        return carry

    lax.fori_loop(0, CHUNKS, drain, 0)
    total = sec_send[dp]
    for p in range(1, DP):
        s_copy(p).wait()
        total = total + sec_recv[p - 1]
    so[...] = total * scale


def write_out(ig, gg, fo, so, ig_out, gg_out, fo_out, so_out, sem):
    rows = ig.shape[0] // 2
    copies = [pltpu.make_async_copy(fo, fo_out, sem.at[4])]
    for a in range(2):
        part = pl.ds(a * rows, rows)
        copies.append(pltpu.make_async_copy(ig.at[part], ig_out.at[part], sem.at[a]))
        copies.append(pltpu.make_async_copy(gg.at[part], gg_out.at[part], sem.at[2 + a]))
    for copy in copies:
        copy.start()
    n = G * NB
    gather = (iota((n, NB), 0) // G == iota((n, NB), 1)).astype(F32)
    own = iota((G, 4, n), 0) == iota((G, 4, n), 2) % G
    for g in range(2):
        wide = jnp.where(own, so[4 * g : 4 * g + 4][None], 0.0).reshape(G * 4, n)
        share = jnp.dot(
            wide, gather, precision=lax.Precision.HIGHEST, preferred_element_type=F32
        )
        for i in range(G):
            so_out[g * G + i] = share[4 * i : 4 * i + 4]
    for copy in copies:
        copy.wait()


def local(tokens, gate, cotangent, first_factor, second_factor):
    seqs, rows, width = tokens.shape
    scale = 1.0 / math.sqrt(width * seqs * DP)
    cw = width // CHUNKS
    flat = (rows, width)
    vm = pltpu.VMEM
    dma = pltpu.SemaphoreType.DMA
    out = (
        vm(flat, BF16), vm(flat, BF16), vm((2, 64, BS), F32), vm((8, G * NB), F32),
    )
    scratch = [
        vm((CHUNKS, rows, cw), BF16), vm((CHUNKS, rows, cw), BF16), vm((CHUNKS, rows, cw), BF16),
        vm((2, BS, BS), BF16), vm((2, BS, BS), BF16), vm((BS * 2, NB), BF16),
        vm((2, BS, BS), BF16), vm((2, BS, BS), BF16),
        vm((CHUNKS, SEQ, 2, 2, G, cw), BF16), vm((CHUNKS, SEQ, 2, 2, G, cw), BF16),
        vm((CHUNKS, 2, NB, G, cw), BF16), vm((CHUNKS, 2, NB, G, cw), BF16),
        vm((2, 4, 2, 64, BS), F32), vm((2, NB, G * NB), F32), vm((3, 2, 2, 64, BS), F32),
        vm((2, 64, BS), BF16), vm((2, 64, BS), BF16), vm((2, 64, BS), F32),
        vm((DP, 8, G * NB), F32), vm((DP - 1, 8, G * NB), F32),
        dma((3, CHUNKS)), dma((2,)),
        dma((CHUNKS,)), dma((CHUNKS,)), dma((CHUNKS,)), dma((CHUNKS,)),
        dma((3,)), dma((3,)), dma, dma, dma((DP - 1,)), dma((DP - 1,)),
    ]
    hbm = pl.BlockSpec(memory_space=pl.ANY)
    inner = pl.BlockSpec(memory_space=pltpu.VMEM)
    ig, gg, fo, so = pl.pallas_call(
        functools.partial(kernel, width, scale),
        out_shape=out,
        in_specs=[hbm] * 5,
        out_specs=[inner] * 4,
        scratch_shapes=scratch,
        compiler_params=pltpu.CompilerParams(
            collective_id=0, has_side_effects=True, vmem_limit_bytes=52 * 2**20
        ),
        cost_estimate=pl.CostEstimate(
            flops=15 * 2**30, bytes_accessed=22 * 2**20, transcendentals=0
        ),
        name="mixer",
    )(
        tokens.reshape(flat), gate.reshape(flat), cotangent.reshape(flat),
        first_factor, second_factor.reshape(BS * 2, NB),
    )
    ig, gg, fo, so = pl.pallas_call(
        write_out,
        out_shape=(
            jax.ShapeDtypeStruct(flat, BF16), jax.ShapeDtypeStruct(flat, BF16),
            jax.ShapeDtypeStruct((2, 64, BS), F32), jax.ShapeDtypeStruct((NB, 4, NB), F32),
        ),
        in_specs=[inner] * 4,
        out_specs=[hbm] * 3 + [inner],
        scratch_shapes=[dma((5,))],
        compiler_params=pltpu.CompilerParams(vmem_limit_bytes=8 * 2**20),
        name="write_out",
    )(ig, gg, fo, so)
    return (ig.reshape(seqs, rows, width), gg.reshape(seqs, rows, width), fo, so)


def solution(mesh):
    placed = (
        P("dp", "seq", None),
        P("dp", "seq", None),
        P("dp", "seq", None),
        P("seq", None, None),
        P("seq", None, None),
    )
    return jax.shard_map(
        local,
        mesh=mesh,
        in_specs=placed,
        out_specs=(
            P("dp", "seq", None),
            P("dp", "seq", None),
            P("seq", "dp", None),
            P("seq", "dp", None),
        ),
        check_vma=False,
    )
```

```python
import functools
import math

import jax
import jax.numpy as jnp
from jax import lax
from jax.experimental import pallas as pl
from jax.experimental.pallas import tpu as pltpu
from jax.sharding import PartitionSpec as P

MESH = pl.DeviceIdType.MESH
F32, BF16 = jnp.float32, jnp.bfloat16
CHUNKS = 16
SEQ, DP = 16, 8
NB, BS, G = 32, 512, 16
NT = (((1,), (1,)), ((), ()))


def iota(shape, dim):
    return lax.broadcasted_iota(jnp.int32, shape, dim)


def kernel(
    width, scale,
    tok, gate, cot, first, second,
    ig, gg, fo, so,
    tok_v, cot_v, mg_v, f_v, ft_v, s_v, w_v, wt_v,
    hg_send, h_send, hg_recv, h_recv,
    facc, sacc, zrecv, xsend, xrecv, xkeep, sec_send, sec_recv,
    load_sem, fac_sem, hg_ss, hg_rs, h_ss, h_rs, z_ss, z_rs, x_ss, x_rs, s_ss, s_rs,
):
    cw = width // CHUNKS
    dp, me = lax.axis_index("dp"), lax.axis_index("seq")
    z, xl = dp // 2, dp % 2

    def chunk_loads(k):
        cols = pl.ds(pl.multiple_of(k * cw, cw), cw)
        return (
            (cot.at[:, cols], cot_v.at[k], load_sem.at[0, k]),
            (gate.at[:, cols], mg_v.at[k], load_sem.at[1, k]),
            (tok.at[:, cols], tok_v.at[k], load_sem.at[2, k]),
        )

    def start_loads(k, which):
        for a in which:
            pltpu.make_async_copy(*chunk_loads(k)[a]).start()

    def wait_loads(k, which):
        for a in which:
            pltpu.make_async_copy(*chunk_loads(k)[a]).wait()

    load_second = pltpu.make_async_copy(second, s_v, fac_sem.at[0])
    load_first = pltpu.make_async_copy(first, f_v, fac_sem.at[1])
    load_first.start()
    start_loads(0, (2,))
    load_second.start()
    start_loads(0, (0, 1))

    barrier = pltpu.get_barrier_semaphore()

    def greet_seq(p, carry):
        pl.semaphore_signal(barrier, inc=1, device_id=(dp, (me + p) % SEQ), device_id_type=MESH)
        return carry

    def greet_dp(p, carry):
        pl.semaphore_signal(barrier, inc=1, device_id=((dp + p) % DP, me), device_id_type=MESH)
        return carry

    lax.fori_loop(1, SEQ, greet_seq, 0)
    lax.fori_loop(1, DP, greet_dp, 0)

    def send(src, dst, k, ss, rs):
        place = dst.at[k, :, pl.ds(2 * me, 2)]

        def one(p, carry):
            t = (me + p) % SEQ
            pltpu.make_async_remote_copy(
                src_ref=src.at[k, t], dst_ref=place, send_sem=ss.at[k], recv_sem=rs.at[k],
                device_id=(dp, t), device_id_type=MESH,
            ).start()
            return carry

        lax.fori_loop(1, SEQ, one, 0)
        pltpu.make_async_copy(src.at[k, me], place, rs.at[k]).start()

    def wait_sent(src, k, ss):
        ref = src.at[k, pl.ds(0, SEQ - 1)]
        pltpu.make_async_copy(ref, ref, ss.at[k]).wait()

    def wait_all(dst, k, rs):
        pltpu.make_async_copy(dst.at[k], dst.at[k], rs.at[k]).wait()

    def make_h(k):
        wait_loads(k, (2,))
        for b in range(2):
            h = jnp.dot(f_v[b], tok_v[k, b * BS : (b + 1) * BS, :], preferred_element_type=F32)
            h_send[k, :, :, b] = h.astype(BF16).reshape(SEQ, 2, G, cw)

    load_first.wait()
    make_h(0)
    pl.semaphore_wait(barrier, SEQ - 1 + DP - 1)
    send(h_send, h_recv, 0, h_ss, h_rs)
    start_loads(1, (0, 1))

    load_second.wait()
    n = G * NB
    spread = (iota((n, NB), 0) // G == iota((n, NB), 1)).astype(BF16)
    same = iota((n, n), 0) // NB == iota((n, n), 1) % G
    same_t = iota((n, n), 1) // NB == iota((n, n), 0) % G
    for g in range(2):
        wt = lax.dot_general(
            spread, s_v[g * n : (g + 1) * n, :], NT, preferred_element_type=F32
        )
        wt_v[g] = jnp.where(same_t, wt, 0.0).astype(BF16)

    def make_hg(k):
        wait_loads(k, (0, 1))
        for g in range(2):
            rows = slice(g * n, (g + 1) * n)
            m = (cot_v[k, rows, :].astype(F32) * mg_v[k, rows, :].astype(F32)).astype(BF16)
            mg_v[k, rows, :] = m
            hg = jnp.dot(wt_v[g], m, preferred_element_type=F32).astype(BF16)
            hg_send[k, :, :, g] = hg.reshape(SEQ, 2, G, cw)

    start_loads(2, (0, 1))

    def hg_step(k, carry):
        @pl.when(k < CHUNKS - 3)
        def _():
            start_loads(k + 3, (0, 1))

        make_hg(k)
        send(hg_send, hg_recv, k, hg_ss, hg_rs)
        return carry

    lax.fori_loop(0, CHUNKS, hg_step, 0)

    def load_tok(k, carry):
        start_loads(k, (2,))
        return carry

    lax.fori_loop(1, CHUNKS, load_tok, 0)
    for g in range(2):
        w = lax.dot_general(
            s_v[g * n : (g + 1) * n, :], spread, NT, preferred_element_type=F32
        )
        w_v[g] = jnp.where(same, w, 0.0).astype(BF16)

    def h_step(k, carry):
        make_h(k)
        return carry

    lax.fori_loop(1, CHUNKS, h_step, 0)
    for b in range(2):
        ft_v[b] = f_v[b].T

    facc[...] = jnp.zeros_like(facc)
    sacc[...] = jnp.zeros_like(sacc)

    def back_step(k, carry):
        wait_sent(hg_send, k, hg_ss)

        @pl.when(k < CHUNKS - 1)
        def _():
            send(h_send, h_recv, k + 1, h_ss, h_rs)

        wait_all(hg_recv, k, hg_rs)
        cols = pl.ds(pl.multiple_of(k * cw, cw), cw)
        for b in range(2):
            hg = hg_recv[k, b].reshape(BS, cw)
            rows = slice(b * BS, (b + 1) * BS)
            ig[rows, cols] = jnp.dot(ft_v[b], hg, preferred_element_type=F32).astype(BF16)
            terms = lax.dot_general(hg, tok_v[k, rows, :], NT, preferred_element_type=F32)
            facc[b] += terms.reshape(4, 2, 64, BS)
        return carry

    lax.fori_loop(0, CHUNKS, back_step, 0)

    def z_copy(d):
        t = (z + d) % 4
        return pltpu.make_async_remote_copy(
            src_ref=facc.at[:, t], dst_ref=zrecv.at[d - 1],
            send_sem=z_ss.at[d - 1], recv_sem=z_rs.at[d - 1],
            device_id=(t * 2 + xl, me), device_id_type=MESH,
        )

    x_copy = pltpu.make_async_remote_copy(
        src_ref=xsend, dst_ref=xrecv, send_sem=x_ss, recv_sem=x_rs,
        device_id=(z * 2 + 1 - xl, me), device_id_type=MESH,
    )
    for d in (1, 2, 3):
        z_copy(d).start()

    def second_terms(k):
        for g in range(2):
            h = h_recv[k, g].reshape(n, cw)
            m = mg_v[k, g * n : (g + 1) * n, :]
            terms = lax.dot_general(m, h, NT, preferred_element_type=F32)
            terms = jnp.where(same, terms, 0.0).reshape(G, NB, n)
            sacc[g] += jnp.sum(terms, axis=0)

    def gate_part(k):
        cols = pl.ds(pl.multiple_of(k * cw, cw), cw)
        for g in range(2):
            h = h_recv[k, g].reshape(n, cw)
            rows = slice(g * n, (g + 1) * n)
            mixed = jnp.dot(w_v[g], h, preferred_element_type=F32)
            gg[rows, cols] = (cot_v[k, rows, :].astype(F32) * mixed).astype(BF16)

    def forth_step(k, carry):
        wait_all(h_recv, k, h_rs)
        second_terms(k)
        gate_part(k)
        return carry

    half = CHUNKS // 2
    lax.fori_loop(0, half, forth_step, 0)

    for d in (1, 2, 3):
        z_copy(d).wait()
    for b in range(2):
        other = facc[b, z, 1 - xl] + zrecv[0, b, 1 - xl] + zrecv[1, b, 1 - xl] + zrecv[2, b, 1 - xl]
        xsend[b] = other.astype(BF16)
    x_copy.start()
    for b in range(2):
        xkeep[b] = facc[b, z, xl] + zrecv[0, b, xl] + zrecv[1, b, xl] + zrecv[2, b, xl]

    lax.fori_loop(half, CHUNKS - 1, forth_step, 0)
    wait_all(h_recv, CHUNKS - 1, h_rs)
    second_terms(CHUNKS - 1)
    for g in range(2):
        for d in range(DP):
            sec_send[d, 4 * g : 4 * g + 4] = sacc[g, 4 * d : 4 * d + 4]

    order = ((2, 1), (1, 1), (3, 1), (2, 0), (1, 0), (3, 0), (0, 1))

    def s_copy(p):
        dz, dx = order[p]
        t = (z + dz) % 4 * 2 + (xl + dx) % 2
        return pltpu.make_async_remote_copy(
            src_ref=sec_send.at[t], dst_ref=sec_recv.at[p],
            send_sem=s_ss.at[p], recv_sem=s_rs.at[p],
            device_id=(t, me), device_id_type=MESH,
        )

    for p in range(DP - 1):
        s_copy(p).start()
    gate_part(CHUNKS - 1)
    x_copy.wait()
    fo[...] = (xkeep[...] + xrecv[...].astype(F32)) * scale

    def drain(k, carry):
        wait_sent(h_send, k, h_ss)
        return carry

    lax.fori_loop(0, CHUNKS, drain, 0)
    total = sec_send[dp]
    for p in reversed(range(DP - 1)):
        s_copy(p).wait()
        total = total + sec_recv[p]
    so[...] = total * scale


def write_out(ig, gg, fo, so, ig_out, gg_out, fo_out, so_out, sem):
    rows = ig.shape[0] // 2
    copies = [pltpu.make_async_copy(fo, fo_out, sem.at[4])]
    for a in range(2):
        part = pl.ds(a * rows, rows)
        copies.append(pltpu.make_async_copy(ig.at[part], ig_out.at[part], sem.at[a]))
        copies.append(pltpu.make_async_copy(gg.at[part], gg_out.at[part], sem.at[2 + a]))
    for copy in copies:
        copy.start()
    n = G * NB
    gather = (iota((n, NB), 0) // G == iota((n, NB), 1)).astype(F32)
    own = iota((G, 4, n), 0) == iota((G, 4, n), 2) % G
    for g in range(2):
        wide = jnp.where(own, so[4 * g : 4 * g + 4][None], 0.0).reshape(G * 4, n)
        share = jnp.dot(
            wide, gather, precision=lax.Precision.HIGHEST, preferred_element_type=F32
        )
        for i in range(G):
            so_out[g * G + i] = share[4 * i : 4 * i + 4]
    for copy in copies:
        copy.wait()


def local(tokens, gate, cotangent, first_factor, second_factor):
    seqs, rows, width = tokens.shape
    scale = 1.0 / math.sqrt(width * seqs * DP)
    cw = width // CHUNKS
    flat = (rows, width)
    vm = pltpu.VMEM
    dma = pltpu.SemaphoreType.DMA
    out = (
        vm(flat, BF16), vm(flat, BF16), vm((2, 64, BS), F32), vm((8, G * NB), F32),
    )
    scratch = [
        vm((CHUNKS, rows, cw), BF16), vm((CHUNKS, rows, cw), BF16), vm((CHUNKS, rows, cw), BF16),
        vm((2, BS, BS), BF16), vm((2, BS, BS), BF16), vm((BS * 2, NB), BF16),
        vm((2, BS, BS), BF16), vm((2, BS, BS), BF16),
        vm((CHUNKS, SEQ, 2, 2, G, cw), BF16), vm((CHUNKS, SEQ, 2, 2, G, cw), BF16),
        vm((CHUNKS, 2, NB, G, cw), BF16), vm((CHUNKS, 2, NB, G, cw), BF16),
        vm((2, 4, 2, 64, BS), F32), vm((2, NB, G * NB), F32), vm((3, 2, 2, 64, BS), F32),
        vm((2, 64, BS), BF16), vm((2, 64, BS), BF16), vm((2, 64, BS), F32),
        vm((DP, 8, G * NB), F32), vm((DP - 1, 8, G * NB), F32),
        dma((3, CHUNKS)), dma((2,)),
        dma((CHUNKS,)), dma((CHUNKS,)), dma((CHUNKS,)), dma((CHUNKS,)),
        dma((3,)), dma((3,)), dma, dma, dma((DP - 1,)), dma((DP - 1,)),
    ]
    hbm = pl.BlockSpec(memory_space=pl.ANY)
    inner = pl.BlockSpec(memory_space=pltpu.VMEM)
    ig, gg, fo, so = pl.pallas_call(
        functools.partial(kernel, width, scale),
        out_shape=out,
        in_specs=[hbm] * 5,
        out_specs=[inner] * 4,
        scratch_shapes=scratch,
        compiler_params=pltpu.CompilerParams(
            collective_id=0, has_side_effects=True, vmem_limit_bytes=52 * 2**20
        ),
        cost_estimate=pl.CostEstimate(
            flops=15 * 2**30, bytes_accessed=22 * 2**20, transcendentals=0
        ),
        name="mixer",
    )(
        tokens.reshape(flat), gate.reshape(flat), cotangent.reshape(flat),
        first_factor, second_factor.reshape(BS * 2, NB),
    )
    ig, gg, fo, so = pl.pallas_call(
        write_out,
        out_shape=(
            jax.ShapeDtypeStruct(flat, BF16), jax.ShapeDtypeStruct(flat, BF16),
            jax.ShapeDtypeStruct((2, 64, BS), F32), jax.ShapeDtypeStruct((NB, 4, NB), F32),
        ),
        in_specs=[inner] * 4,
        out_specs=[hbm] * 3 + [inner],
        scratch_shapes=[dma((5,))],
        compiler_params=pltpu.CompilerParams(vmem_limit_bytes=8 * 2**20),
        name="write_out",
    )(ig, gg, fo, so)
    return (ig.reshape(seqs, rows, width), gg.reshape(seqs, rows, width), fo, so)


def solution(mesh):
    placed = (
        P("dp", "seq", None),
        P("dp", "seq", None),
        P("dp", "seq", None),
        P("seq", None, None),
        P("seq", None, None),
    )
    return jax.shard_map(
        local,
        mesh=mesh,
        in_specs=placed,
        out_specs=(
            P("dp", "seq", None),
            P("dp", "seq", None),
            P("seq", "dp", None),
            P("seq", "dp", None),
        ),
        check_vma=False,
    )
```

```python
import functools
import math

import jax
import jax.numpy as jnp
from jax import lax
from jax.experimental import pallas as pl
from jax.experimental.pallas import tpu as pltpu
from jax.sharding import PartitionSpec as P

MESH = pl.DeviceIdType.MESH
F32, BF16 = jnp.float32, jnp.bfloat16
WINDOW = 16
CHUNKS = 16
SEQ, DP = 16, 8
NB, BS, G = 32, 512, 16
NT = (((1,), (1,)), ((), ()))


def iota(shape, dim):
    return lax.broadcasted_iota(jnp.int32, shape, dim)


def kernel(
    width, scale,
    tok, gate, cot, first, second,
    ig, gg, fo, so,
    tok_v, cot_v, mg_v, f_v, ft_v, s_v, w_v, wt_v,
    hg_send, h_send, hg_recv, h_recv,
    facc, sacc, zrecv, xsend, xrecv, xkeep, sec_send, sec_recv,
    load_sem, fac_sem, hg_ss, hg_rs, h_ss, h_rs, z_ss, z_rs, x_ss, x_rs, s_ss, s_rs,
):
    cw = width // CHUNKS
    dp, me = lax.axis_index("dp"), lax.axis_index("seq")
    z, xl = dp // 2, dp % 2

    def chunk_loads(k):
        cols = pl.ds(pl.multiple_of(k * cw, cw), cw)
        return (
            (cot.at[:, cols], cot_v.at[k], load_sem.at[0, k]),
            (gate.at[:, cols], mg_v.at[k], load_sem.at[1, k]),
            (tok.at[:, cols], tok_v.at[k], load_sem.at[2, k]),
        )

    def start_loads(k, which):
        for a in which:
            pltpu.make_async_copy(*chunk_loads(k)[a]).start()

    def wait_loads(k, which):
        for a in which:
            pltpu.make_async_copy(*chunk_loads(k)[a]).wait()

    load_second = pltpu.make_async_copy(second, s_v, fac_sem.at[0])
    load_first = pltpu.make_async_copy(first, f_v, fac_sem.at[1])
    load_first.start()
    start_loads(0, (2,))
    load_second.start()
    start_loads(0, (0, 1))

    barrier = pltpu.get_barrier_semaphore()

    def greet_seq(p, carry):
        pl.semaphore_signal(barrier, inc=1, device_id=(dp, (me + p) % SEQ), device_id_type=MESH)
        return carry

    def greet_dp(p, carry):
        pl.semaphore_signal(barrier, inc=1, device_id=((dp + p) % DP, me), device_id_type=MESH)
        return carry

    lax.fori_loop(1, SEQ, greet_seq, 0)
    lax.fori_loop(1, DP, greet_dp, 0)

    def send(src, dst, k, ss, rs):
        place = dst.at[k, me]

        def one(p, carry):
            t = (me + p) % SEQ
            pltpu.make_async_remote_copy(
                src_ref=src.at[k, t], dst_ref=place, send_sem=ss.at[k], recv_sem=rs.at[k],
                device_id=(dp, t), device_id_type=MESH,
            ).start()
            return carry

        lax.fori_loop(1, SEQ, one, 0)
        pltpu.make_async_copy(src.at[k, me], place, rs.at[k]).start()

    def wait_sent(src, k, ss):
        ref = src.at[k, pl.ds(0, SEQ - 1)]
        pltpu.make_async_copy(ref, ref, ss.at[k]).wait()

    def wait_all(dst, k, rs):
        pltpu.make_async_copy(dst.at[k], dst.at[k], rs.at[k]).wait()

    def make_h(k):
        wait_loads(k, (2,))
        for b in range(2):
            h = jnp.dot(f_v[b], tok_v[k, b * BS : (b + 1) * BS, :], preferred_element_type=F32)
            h_send[k, :, :, b] = h.astype(BF16).reshape(SEQ, 2, G, cw)

    load_first.wait()
    make_h(0)
    pl.semaphore_wait(barrier, SEQ - 1 + DP - 1)
    send(h_send, h_recv, 0, h_ss, h_rs)
    start_loads(1, (0, 1))

    load_second.wait()
    n = G * NB
    spread = (iota((n, NB), 0) // G == iota((n, NB), 1)).astype(BF16)
    same = iota((n, n), 0) // NB == iota((n, n), 1) % G
    same_t = iota((n, n), 1) // NB == iota((n, n), 0) % G
    for g in range(2):
        wt = lax.dot_general(
            spread, s_v[g * n : (g + 1) * n, :], NT, preferred_element_type=F32
        )
        wt_v[g] = jnp.where(same_t, wt, 0.0).astype(BF16)

    def make_hg(k):
        wait_loads(k, (0, 1))
        for g in range(2):
            rows = slice(g * n, (g + 1) * n)
            m = (cot_v[k, rows, :].astype(F32) * mg_v[k, rows, :].astype(F32)).astype(BF16)
            mg_v[k, rows, :] = m
            hg = jnp.dot(wt_v[g], m, preferred_element_type=F32).astype(BF16)
            hg_send[k, :, :, g] = hg.reshape(SEQ, 2, G, cw)

    start_loads(2, (0, 1))

    def load_pair(k):
        @pl.when(k < CHUNKS - 3)
        def _():
            start_loads(k + 3, (0, 1))

    def hg_first(k, carry):
        load_pair(k)
        make_hg(k)
        send(hg_send, hg_recv, k, hg_ss, hg_rs)
        return carry

    def hg_rest(k, carry):
        load_pair(k)
        make_hg(k)
        return carry

    lax.fori_loop(0, WINDOW - 1, hg_first, 0)
    lax.fori_loop(WINDOW - 1, CHUNKS, hg_rest, 0)

    def start_item(n):
        @pl.when(n <= CHUNKS)
        def _():
            send(hg_send, hg_recv, n - 1, hg_ss, hg_rs)

        @pl.when((n > CHUNKS) & (n < 2 * CHUNKS))
        def _():
            send(h_send, h_recv, n - CHUNKS, h_ss, h_rs)

    def wait_item(n):
        @pl.when((n > 0) & (n <= CHUNKS))
        def _():
            wait_sent(hg_send, n - 1, hg_ss)

        @pl.when(n > CHUNKS)
        def _():
            wait_sent(h_send, n - CHUNKS, h_ss)

        @pl.when(n == 0)
        def _():
            wait_sent(h_send, 0, h_ss)

    def next_item(n):
        wait_item(n)
        start_item(n + WINDOW)

    def load_tok(k, carry):
        start_loads(k, (2,))
        return carry

    lax.fori_loop(1, CHUNKS, load_tok, 0)
    for g in range(2):
        w = lax.dot_general(
            s_v[g * n : (g + 1) * n, :], spread, NT, preferred_element_type=F32
        )
        w_v[g] = jnp.where(same, w, 0.0).astype(BF16)

    def h_step(k, carry):
        make_h(k)
        return carry

    lax.fori_loop(1, CHUNKS, h_step, 0)
    for b in range(2):
        ft_v[b] = f_v[b].T

    facc[...] = jnp.zeros_like(facc)
    sacc[...] = jnp.zeros_like(sacc)

    def back_step(k, carry):
        next_item(k)
        wait_all(hg_recv, k, hg_rs)
        cols = pl.ds(pl.multiple_of(k * cw, cw), cw)
        for b in range(2):
            hg = hg_recv[k, :, b].reshape(BS, cw)
            rows = slice(b * BS, (b + 1) * BS)
            ig[rows, cols] = jnp.dot(ft_v[b], hg, preferred_element_type=F32).astype(BF16)
            terms = lax.dot_general(hg, tok_v[k, rows, :], NT, preferred_element_type=F32)
            facc[b] += terms.reshape(4, 2, 64, BS)
        return carry

    lax.fori_loop(0, CHUNKS, back_step, 0)

    def z_copy(d):
        t = (z + d) % 4
        return pltpu.make_async_remote_copy(
            src_ref=facc.at[:, t], dst_ref=zrecv.at[d - 1],
            send_sem=z_ss.at[d - 1], recv_sem=z_rs.at[d - 1],
            device_id=(t * 2 + xl, me), device_id_type=MESH,
        )

    x_copy = pltpu.make_async_remote_copy(
        src_ref=xsend, dst_ref=xrecv, send_sem=x_ss, recv_sem=x_rs,
        device_id=(z * 2 + 1 - xl, me), device_id_type=MESH,
    )
    for d in (1, 2, 3):
        z_copy(d).start()

    def second_terms(k):
        for g in range(2):
            h = h_recv[k, :, g].reshape(n, cw)
            m = mg_v[k, g * n : (g + 1) * n, :]
            terms = lax.dot_general(m, h, NT, preferred_element_type=F32)
            terms = jnp.where(same, terms, 0.0).reshape(G, NB, n)
            sacc[g] += jnp.sum(terms, axis=0)

    def gate_part(k):
        cols = pl.ds(pl.multiple_of(k * cw, cw), cw)
        for g in range(2):
            h = h_recv[k, :, g].reshape(n, cw)
            rows = slice(g * n, (g + 1) * n)
            mixed = jnp.dot(w_v[g], h, preferred_element_type=F32)
            gg[rows, cols] = (cot_v[k, rows, :].astype(F32) * mixed).astype(BF16)

    def forth_step(k, carry):
        next_item(k + CHUNKS)
        wait_all(h_recv, k, h_rs)
        second_terms(k)
        gate_part(k)
        return carry

    half = CHUNKS // 2
    lax.fori_loop(0, half, forth_step, 0)

    for d in (1, 2, 3):
        z_copy(d).wait()
    for b in range(2):
        other = facc[b, z, 1 - xl] + zrecv[0, b, 1 - xl] + zrecv[1, b, 1 - xl] + zrecv[2, b, 1 - xl]
        xsend[b] = other.astype(BF16)
    x_copy.start()
    for b in range(2):
        xkeep[b] = facc[b, z, xl] + zrecv[0, b, xl] + zrecv[1, b, xl] + zrecv[2, b, xl]

    lax.fori_loop(half, CHUNKS - 1, forth_step, 0)
    wait_all(h_recv, CHUNKS - 1, h_rs)
    second_terms(CHUNKS - 1)
    for g in range(2):
        for d in range(DP):
            sec_send[d, 4 * g : 4 * g + 4] = sacc[g, 4 * d : 4 * d + 4]

    order = ((2, 1), (1, 1), (3, 1), (2, 0), (1, 0), (3, 0), (0, 1))

    def s_copy(p):
        dz, dx = order[p]
        t = (z + dz) % 4 * 2 + (xl + dx) % 2
        return pltpu.make_async_remote_copy(
            src_ref=sec_send.at[t], dst_ref=sec_recv.at[p],
            send_sem=s_ss.at[p], recv_sem=s_rs.at[p],
            device_id=(t, me), device_id_type=MESH,
        )

    for p in range(DP - 1):
        s_copy(p).start()
    gate_part(CHUNKS - 1)
    x_copy.wait()
    fo[...] = (xkeep[...] + xrecv[...].astype(F32)) * scale

    wait_item(2 * CHUNKS - 1)
    total = sec_send[dp]
    for p in reversed(range(DP - 1)):
        s_copy(p).wait()
        total = total + sec_recv[p]
    so[...] = total * scale


def write_out(ig, gg, fo, so, ig_out, gg_out, fo_out, so_out, so_v, sem):
    rows = ig.shape[0] // 2
    copies = [pltpu.make_async_copy(fo, fo_out, sem.at[4])]
    for a in range(2):
        part = pl.ds(a * rows, rows)
        copies.append(pltpu.make_async_copy(ig.at[part], ig_out.at[part], sem.at[a]))
        copies.append(pltpu.make_async_copy(gg.at[part], gg_out.at[part], sem.at[2 + a]))
    for copy in copies:
        copy.start()
    n = G * NB
    gather = (iota((n, NB), 0) // G == iota((n, NB), 1)).astype(F32)
    own = iota((G, 4, n), 0) == iota((G, 4, n), 2) % G
    for g in range(2):
        wide = jnp.where(own, so[4 * g : 4 * g + 4][None], 0.0).reshape(G * 4, n)
        share = jnp.dot(
            wide, gather, precision=lax.Precision.HIGHEST, preferred_element_type=F32
        )
        for i in range(G):
            so_v[g * G + i] = share[4 * i : 4 * i + 4]
    copies.append(pltpu.make_async_copy(so_v, so_out, sem.at[5]))
    copies[-1].start()
    for copy in copies:
        copy.wait()


def local(tokens, gate, cotangent, first_factor, second_factor):
    seqs, rows, width = tokens.shape
    scale = 1.0 / math.sqrt(width * seqs * DP)
    cw = width // CHUNKS
    flat = (rows, width)
    vm = pltpu.VMEM
    dma = pltpu.SemaphoreType.DMA
    out = (
        vm(flat, BF16), vm(flat, BF16), vm((2, 64, BS), F32), vm((8, G * NB), F32),
    )
    scratch = [
        vm((CHUNKS, rows, cw), BF16), vm((CHUNKS, rows, cw), BF16), vm((CHUNKS, rows, cw), BF16),
        vm((2, BS, BS), BF16), vm((2, BS, BS), BF16), vm((BS * 2, NB), BF16),
        vm((2, BS, BS), BF16), vm((2, BS, BS), BF16),
        vm((CHUNKS, SEQ, 2, 2, G, cw), BF16), vm((CHUNKS, SEQ, 2, 2, G, cw), BF16),
        vm((CHUNKS, SEQ, 2, 2, G, cw), BF16), vm((CHUNKS, SEQ, 2, 2, G, cw), BF16),
        vm((2, 4, 2, 64, BS), F32), vm((2, NB, G * NB), F32), vm((3, 2, 2, 64, BS), F32),
        vm((2, 64, BS), BF16), vm((2, 64, BS), BF16), vm((2, 64, BS), F32),
        vm((DP, 8, G * NB), F32), vm((DP - 1, 8, G * NB), F32),
        dma((3, CHUNKS)), dma((2,)),
        dma((CHUNKS,)), dma((CHUNKS,)), dma((CHUNKS,)), dma((CHUNKS,)),
        dma((3,)), dma((3,)), dma, dma, dma((DP - 1,)), dma((DP - 1,)),
    ]
    hbm = pl.BlockSpec(memory_space=pl.ANY)
    inner = pl.BlockSpec(memory_space=pltpu.VMEM)
    ig, gg, fo, so = pl.pallas_call(
        functools.partial(kernel, width, scale),
        out_shape=out,
        in_specs=[hbm] * 5,
        out_specs=[inner] * 4,
        scratch_shapes=scratch,
        compiler_params=pltpu.CompilerParams(
            collective_id=0, has_side_effects=True, vmem_limit_bytes=52 * 2**20
        ),
        cost_estimate=pl.CostEstimate(
            flops=15 * 2**30, bytes_accessed=22 * 2**20, transcendentals=0
        ),
        name="mixer",
    )(
        tokens.reshape(flat), gate.reshape(flat), cotangent.reshape(flat),
        first_factor, second_factor.reshape(BS * 2, NB),
    )
    ig, gg, fo, so = pl.pallas_call(
        write_out,
        out_shape=(
            jax.ShapeDtypeStruct(flat, BF16), jax.ShapeDtypeStruct(flat, BF16),
            jax.ShapeDtypeStruct((2, 64, BS), F32), jax.ShapeDtypeStruct((NB, 4, NB), F32),
        ),
        in_specs=[inner] * 4,
        out_specs=[hbm] * 4,
        scratch_shapes=[vm((NB, 4, NB), F32), dma((6,))],
        compiler_params=pltpu.CompilerParams(vmem_limit_bytes=8 * 2**20),
        name="write_out",
    )(ig, gg, fo, so)
    return (ig.reshape(seqs, rows, width), gg.reshape(seqs, rows, width), fo, so)


def solution(mesh):
    placed = (
        P("dp", "seq", None),
        P("dp", "seq", None),
        P("dp", "seq", None),
        P("seq", None, None),
        P("seq", None, None),
    )
    return jax.shard_map(
        local,
        mesh=mesh,
        in_specs=placed,
        out_specs=(
            P("dp", "seq", None),
            P("dp", "seq", None),
            P("seq", "dp", None),
            P("seq", "dp", None),
        ),
        check_vma=False,
    )
```

```python
import functools
import math

import jax
import jax.numpy as jnp
from jax import lax
from jax.experimental import pallas as pl
from jax.experimental.pallas import tpu as pltpu
from jax.sharding import PartitionSpec as P

MESH = pl.DeviceIdType.MESH
F32, BF16 = jnp.float32, jnp.bfloat16
WINDOW = 16
CHUNKS = 16
SEQ, DP = 16, 8
NB, BS, G = 32, 512, 16
NT = (((1,), (1,)), ((), ()))


def iota(shape, dim):
    return lax.broadcasted_iota(jnp.int32, shape, dim)


def kernel(
    width, scale,
    tok, gate, cot, first, second,
    ig, gg, fo, so,
    tok_v, cot_v, mg_v, f_v, ft_v, s_v, w_v, wt_v,
    hg_send, h_send, hg_recv, h_recv,
    facc, sacc, zrecv, xsend, xrecv, xkeep, sec_send, sec_recv,
    load_sem, fac_sem, hg_ss, hg_rs, h_ss, h_rs, z_ss, z_rs, x_ss, x_rs, s_ss, s_rs,
):
    cw = width // CHUNKS
    dp, me = lax.axis_index("dp"), lax.axis_index("seq")
    z, xl = dp // 2, dp % 2

    def chunk_loads(k):
        cols = pl.ds(pl.multiple_of(k * cw, cw), cw)
        return (
            (cot.at[:, cols], cot_v.at[k], load_sem.at[0, k]),
            (gate.at[:, cols], mg_v.at[k], load_sem.at[1, k]),
            (tok.at[:, cols], tok_v.at[k], load_sem.at[2, k]),
        )

    def start_loads(k, which):
        for a in which:
            pltpu.make_async_copy(*chunk_loads(k)[a]).start()

    def wait_loads(k, which):
        for a in which:
            pltpu.make_async_copy(*chunk_loads(k)[a]).wait()

    load_second = pltpu.make_async_copy(second, s_v, fac_sem.at[0])
    load_first = pltpu.make_async_copy(first, f_v, fac_sem.at[1])
    load_first.start()
    start_loads(0, (2,))
    load_second.start()
    start_loads(0, (0, 1))

    barrier = pltpu.get_barrier_semaphore()

    def greet_seq(p, carry):
        pl.semaphore_signal(barrier, inc=1, device_id=(dp, (me + p) % SEQ), device_id_type=MESH)
        return carry

    def greet_dp(p, carry):
        pl.semaphore_signal(barrier, inc=1, device_id=((dp + p) % DP, me), device_id_type=MESH)
        return carry

    lax.fori_loop(1, SEQ, greet_seq, 0)
    lax.fori_loop(1, DP, greet_dp, 0)

    def send(src, dst, k, ss, rs):
        place = dst.at[k, me]

        def one(p, carry):
            t = (me + p) % SEQ
            pltpu.make_async_remote_copy(
                src_ref=src.at[k, t], dst_ref=place, send_sem=ss.at[k], recv_sem=rs.at[k],
                device_id=(dp, t), device_id_type=MESH,
            ).start()
            return carry

        lax.fori_loop(1, SEQ, one, 0)
        pltpu.make_async_copy(src.at[k, me], place, rs.at[k]).start()

    def wait_sent(src, k, ss):
        ref = src.at[k, pl.ds(0, SEQ - 1)]
        pltpu.make_async_copy(ref, ref, ss.at[k]).wait()

    def wait_all(dst, k, rs):
        pltpu.make_async_copy(dst.at[k], dst.at[k], rs.at[k]).wait()

    def make_h(k):
        wait_loads(k, (2,))
        for b in range(2):
            h = jnp.dot(f_v[b], tok_v[k, b * BS : (b + 1) * BS, :], preferred_element_type=F32)
            h_send[k, :, :, b] = h.astype(BF16).reshape(SEQ, 2, G, cw)

    load_first.wait()
    make_h(0)
    pl.semaphore_wait(barrier, SEQ - 1 + DP - 1)
    send(h_send, h_recv, 0, h_ss, h_rs)
    start_loads(1, (0, 1))

    load_second.wait()
    n = G * NB
    spread = (iota((n, NB), 0) // G == iota((n, NB), 1)).astype(BF16)
    same = iota((n, n), 0) // NB == iota((n, n), 1) % G
    same_t = iota((n, n), 1) // NB == iota((n, n), 0) % G
    for g in range(2):
        wt = lax.dot_general(
            spread, s_v[g * n : (g + 1) * n, :], NT, preferred_element_type=F32
        )
        wt_v[g] = jnp.where(same_t, wt, 0.0).astype(BF16)

    def make_hg(k):
        wait_loads(k, (0, 1))
        for g in range(2):
            rows = slice(g * n, (g + 1) * n)
            m = (cot_v[k, rows, :].astype(F32) * mg_v[k, rows, :].astype(F32)).astype(BF16)
            mg_v[k, rows, :] = m
            hg = jnp.dot(wt_v[g], m, preferred_element_type=F32).astype(BF16)
            hg_send[k, :, :, g] = hg.reshape(SEQ, 2, G, cw)

    start_loads(2, (0, 1))

    def load_pair(k):
        @pl.when(k < CHUNKS - 3)
        def _():
            start_loads(k + 3, (0, 1))

    def hg_first(k, carry):
        load_pair(k)
        make_hg(k)
        send(hg_send, hg_recv, k, hg_ss, hg_rs)
        return carry

    def hg_rest(k, carry):
        load_pair(k)
        make_hg(k)
        return carry

    lax.fori_loop(0, WINDOW - 1, hg_first, 0)
    lax.fori_loop(WINDOW - 1, CHUNKS, hg_rest, 0)

    def start_item(n):
        @pl.when(n <= CHUNKS)
        def _():
            send(hg_send, hg_recv, n - 1, hg_ss, hg_rs)

        @pl.when((n > CHUNKS) & (n < 2 * CHUNKS))
        def _():
            send(h_send, h_recv, n - CHUNKS, h_ss, h_rs)

    def wait_item(n):
        @pl.when((n > 0) & (n <= CHUNKS))
        def _():
            wait_sent(hg_send, n - 1, hg_ss)

        @pl.when(n > CHUNKS)
        def _():
            wait_sent(h_send, n - CHUNKS, h_ss)

        @pl.when(n == 0)
        def _():
            wait_sent(h_send, 0, h_ss)

    def next_item(n):
        wait_item(n)
        start_item(n + WINDOW)

    def load_tok(k, carry):
        start_loads(k, (2,))
        return carry

    lax.fori_loop(1, CHUNKS, load_tok, 0)
    for g in range(2):
        w = lax.dot_general(
            s_v[g * n : (g + 1) * n, :], spread, NT, preferred_element_type=F32
        )
        w_v[g] = jnp.where(same, w, 0.0).astype(BF16)

    def h_step(k, carry):
        make_h(k)
        return carry

    lax.fori_loop(1, CHUNKS, h_step, 0)
    for b in range(2):
        ft_v[b] = f_v[b].T

    facc[...] = jnp.zeros_like(facc)
    sacc[...] = jnp.zeros_like(sacc)

    def back_step(k, carry):
        next_item(k)
        wait_all(hg_recv, k, hg_rs)
        cols = pl.ds(pl.multiple_of(k * cw, cw), cw)
        for b in range(2):
            hg = hg_recv[k, :, b].reshape(BS, cw)
            rows = slice(b * BS, (b + 1) * BS)
            ig[rows, cols] = jnp.dot(ft_v[b], hg, preferred_element_type=F32).astype(BF16)
            terms = lax.dot_general(hg, tok_v[k, rows, :], NT, preferred_element_type=F32)
            facc[b] += terms.reshape(4, 2, 64, BS)
        return carry

    lax.fori_loop(0, CHUNKS, back_step, 0)

    def z_copy(d):
        t = (z + d) % 4
        return pltpu.make_async_remote_copy(
            src_ref=facc.at[:, t], dst_ref=zrecv.at[d - 1],
            send_sem=z_ss.at[d - 1], recv_sem=z_rs.at[d - 1],
            device_id=(t * 2 + xl, me), device_id_type=MESH,
        )

    x_copy = pltpu.make_async_remote_copy(
        src_ref=xsend, dst_ref=xrecv, send_sem=x_ss, recv_sem=x_rs,
        device_id=(z * 2 + 1 - xl, me), device_id_type=MESH,
    )
    for d in (1, 2, 3):
        z_copy(d).start()

    def second_terms(k):
        for g in range(2):
            h = h_recv[k, :, g].reshape(n, cw)
            m = mg_v[k, g * n : (g + 1) * n, :]
            terms = lax.dot_general(m, h, NT, preferred_element_type=F32)
            terms = jnp.where(same, terms, 0.0).reshape(G, NB, n)
            sacc[g] += jnp.sum(terms, axis=0)

    def gate_part(k):
        cols = pl.ds(pl.multiple_of(k * cw, cw), cw)
        for g in range(2):
            h = h_recv[k, :, g].reshape(n, cw)
            rows = slice(g * n, (g + 1) * n)
            mixed = jnp.dot(w_v[g], h, preferred_element_type=F32)
            gg[rows, cols] = (cot_v[k, rows, :].astype(F32) * mixed).astype(BF16)

    order = ((2, 1), (1, 1), (3, 1), (2, 0), (1, 0), (3, 0), (0, 1))

    def s_copy(p):
        dz, dx = order[p]
        t = (z + dz) % 4 * 2 + (xl + dx) % 2
        return pltpu.make_async_remote_copy(
            src_ref=sec_send.at[t], dst_ref=sec_recv.at[p],
            send_sem=s_ss.at[p], recv_sem=s_rs.at[p],
            device_id=(t, me), device_id_type=MESH,
        )

    def sum_z():
        for d in (1, 2, 3):
            z_copy(d).wait()
        for b in range(2):
            other = facc[b, z, 1 - xl] + zrecv[0, b, 1 - xl] + zrecv[1, b, 1 - xl] + zrecv[2, b, 1 - xl]
            xsend[b] = other.astype(BF16)
        x_copy.start()
        for b in range(2):
            xkeep[b] = facc[b, z, xl] + zrecv[0, b, xl] + zrecv[1, b, xl] + zrecv[2, b, xl]

    def share_second():
        for g in range(2):
            for d in range(DP):
                sec_send[d, 4 * g : 4 * g + 4] = sacc[g, 4 * d : 4 * d + 4]
        for p in range(DP - 1):
            s_copy(p).start()

    def forth_step(k, carry):
        pl.when(k < CHUNKS - 1)(lambda: next_item(k + CHUNKS))
        wait_all(h_recv, k, h_rs)
        second_terms(k)
        pl.when(k == CHUNKS // 2)(sum_z)
        pl.when(k == CHUNKS - 1)(share_second)
        gate_part(k)
        return carry

    lax.fori_loop(0, CHUNKS, forth_step, 0)
    x_copy.wait()
    fo[...] = (xkeep[...] + xrecv[...].astype(F32)) * scale

    wait_item(2 * CHUNKS - 1)
    total = sec_send[dp]
    for p in reversed(range(DP - 1)):
        s_copy(p).wait()
        total = total + sec_recv[p]
    so[...] = total * scale


def write_out(ig, gg, fo, so, ig_out, gg_out, fo_out, so_out, so_v, sem):
    rows = ig.shape[0] // 2
    copies = [pltpu.make_async_copy(fo, fo_out, sem.at[4])]
    for a in range(2):
        part = pl.ds(a * rows, rows)
        copies.append(pltpu.make_async_copy(ig.at[part], ig_out.at[part], sem.at[a]))
        copies.append(pltpu.make_async_copy(gg.at[part], gg_out.at[part], sem.at[2 + a]))
    for copy in copies:
        copy.start()
    n = G * NB
    gather = (iota((n, NB), 0) // G == iota((n, NB), 1)).astype(F32)
    own = iota((G, 4, n), 0) == iota((G, 4, n), 2) % G
    for g in range(2):
        wide = jnp.where(own, so[4 * g : 4 * g + 4][None], 0.0).reshape(G * 4, n)
        share = jnp.dot(
            wide, gather, precision=lax.Precision.HIGHEST, preferred_element_type=F32
        )
        for i in range(G):
            so_v[g * G + i] = share[4 * i : 4 * i + 4]
    copies.append(pltpu.make_async_copy(so_v, so_out, sem.at[5]))
    copies[-1].start()
    for copy in copies:
        copy.wait()


def local(tokens, gate, cotangent, first_factor, second_factor):
    seqs, rows, width = tokens.shape
    scale = 1.0 / math.sqrt(width * seqs * DP)
    cw = width // CHUNKS
    flat = (rows, width)
    vm = pltpu.VMEM
    dma = pltpu.SemaphoreType.DMA
    out = (
        vm(flat, BF16), vm(flat, BF16), vm((2, 64, BS), F32), vm((8, G * NB), F32),
    )
    scratch = [
        vm((CHUNKS, rows, cw), BF16), vm((CHUNKS, rows, cw), BF16), vm((CHUNKS, rows, cw), BF16),
        vm((2, BS, BS), BF16), vm((2, BS, BS), BF16), vm((BS * 2, NB), BF16),
        vm((2, BS, BS), BF16), vm((2, BS, BS), BF16),
        vm((CHUNKS, SEQ, 2, 2, G, cw), BF16), vm((CHUNKS, SEQ, 2, 2, G, cw), BF16),
        vm((CHUNKS, SEQ, 2, 2, G, cw), BF16), vm((CHUNKS, SEQ, 2, 2, G, cw), BF16),
        vm((2, 4, 2, 64, BS), F32), vm((2, NB, G * NB), F32), vm((3, 2, 2, 64, BS), F32),
        vm((2, 64, BS), BF16), vm((2, 64, BS), BF16), vm((2, 64, BS), F32),
        vm((DP, 8, G * NB), F32), vm((DP - 1, 8, G * NB), F32),
        dma((3, CHUNKS)), dma((2,)),
        dma((CHUNKS,)), dma((CHUNKS,)), dma((CHUNKS,)), dma((CHUNKS,)),
        dma((3,)), dma((3,)), dma, dma, dma((DP - 1,)), dma((DP - 1,)),
    ]
    hbm = pl.BlockSpec(memory_space=pl.ANY)
    inner = pl.BlockSpec(memory_space=pltpu.VMEM)
    ig, gg, fo, so = pl.pallas_call(
        functools.partial(kernel, width, scale),
        out_shape=out,
        in_specs=[hbm] * 5,
        out_specs=[inner] * 4,
        scratch_shapes=scratch,
        compiler_params=pltpu.CompilerParams(
            collective_id=0, has_side_effects=True, vmem_limit_bytes=52 * 2**20
        ),
        cost_estimate=pl.CostEstimate(
            flops=15 * 2**30, bytes_accessed=22 * 2**20, transcendentals=0
        ),
        name="mixer",
    )(
        tokens.reshape(flat), gate.reshape(flat), cotangent.reshape(flat),
        first_factor, second_factor.reshape(BS * 2, NB),
    )
    ig, gg, fo, so = pl.pallas_call(
        write_out,
        out_shape=(
            jax.ShapeDtypeStruct(flat, BF16), jax.ShapeDtypeStruct(flat, BF16),
            jax.ShapeDtypeStruct((2, 64, BS), F32), jax.ShapeDtypeStruct((NB, 4, NB), F32),
        ),
        in_specs=[inner] * 4,
        out_specs=[hbm] * 4,
        scratch_shapes=[vm((NB, 4, NB), F32), dma((6,))],
        compiler_params=pltpu.CompilerParams(vmem_limit_bytes=8 * 2**20),
        name="write_out",
    )(ig, gg, fo, so)
    return (ig.reshape(seqs, rows, width), gg.reshape(seqs, rows, width), fo, so)


def solution(mesh):
    placed = (
        P("dp", "seq", None),
        P("dp", "seq", None),
        P("dp", "seq", None),
        P("seq", None, None),
        P("seq", None, None),
    )
    return jax.shard_map(
        local,
        mesh=mesh,
        in_specs=placed,
        out_specs=(
            P("dp", "seq", None),
            P("dp", "seq", None),
            P("seq", "dp", None),
            P("seq", "dp", None),
        ),
        check_vma=False,
    )
```

```python
import functools
import math

import jax
import jax.numpy as jnp
from jax import lax
from jax.experimental import pallas as pl
from jax.experimental.pallas import tpu as pltpu
from jax.sharding import PartitionSpec as P

MESH = pl.DeviceIdType.MESH
F32, BF16 = jnp.float32, jnp.bfloat16
WINDOW = 16
CHUNKS = 16
SEQ, DP = 16, 8
NB, BS, G = 32, 512, 16
NT = (((1,), (1,)), ((), ()))


def iota(shape, dim):
    return lax.broadcasted_iota(jnp.int32, shape, dim)


def kernel(
    width, scale,
    tok, gate, cot, first, second,
    ig, gg, fo, so,
    tok_v, cot_v, mg_v, f_v, ft_v, s_v, w_v, wt_v,
    hg_send, h_send, hg_recv, h_recv,
    facc, sacc, zrecv, xsend, xrecv, xkeep, sec_own, sec_send, sec_recv,
    load_sem, fac_sem, hg_ss, hg_rs, h_ss, h_rs, z_ss, z_rs, x_ss, x_rs, s_ss, s_rs,
):
    cw = width // CHUNKS
    dp, me = lax.axis_index("dp"), lax.axis_index("seq")
    z, xl = dp // 2, dp % 2

    def chunk_loads(k):
        cols = pl.ds(pl.multiple_of(k * cw, cw), cw)
        return (
            (cot.at[:, cols], cot_v.at[k], load_sem.at[0, k]),
            (gate.at[:, cols], mg_v.at[k], load_sem.at[1, k]),
            (tok.at[:, cols], tok_v.at[k], load_sem.at[2, k]),
        )

    def start_loads(k, which):
        for a in which:
            pltpu.make_async_copy(*chunk_loads(k)[a]).start()

    def wait_loads(k, which):
        for a in which:
            pltpu.make_async_copy(*chunk_loads(k)[a]).wait()

    load_second = pltpu.make_async_copy(second, s_v, fac_sem.at[0])
    load_first = pltpu.make_async_copy(first, f_v, fac_sem.at[1])
    load_first.start()
    start_loads(0, (2,))
    load_second.start()
    start_loads(0, (0, 1))

    barrier = pltpu.get_barrier_semaphore()

    def greet_seq(p, carry):
        pl.semaphore_signal(barrier, inc=1, device_id=(dp, (me + p) % SEQ), device_id_type=MESH)
        return carry

    def greet_dp(p, carry):
        pl.semaphore_signal(barrier, inc=1, device_id=((dp + p) % DP, me), device_id_type=MESH)
        return carry

    lax.fori_loop(1, SEQ, greet_seq, 0)
    lax.fori_loop(1, DP, greet_dp, 0)

    def send(src, dst, k, ss, rs):
        place = dst.at[k, me]

        def one(p, carry):
            t = (me + p) % SEQ
            pltpu.make_async_remote_copy(
                src_ref=src.at[k, t], dst_ref=place, send_sem=ss.at[k], recv_sem=rs.at[k],
                device_id=(dp, t), device_id_type=MESH,
            ).start()
            return carry

        lax.fori_loop(1, SEQ, one, 0)
        pltpu.make_async_copy(src.at[k, me], place, rs.at[k]).start()

    def wait_sent(src, k, ss):
        ref = src.at[k, pl.ds(0, SEQ - 1)]
        pltpu.make_async_copy(ref, ref, ss.at[k]).wait()

    def wait_all(dst, k, rs):
        pltpu.make_async_copy(dst.at[k], dst.at[k], rs.at[k]).wait()

    def make_h(k):
        wait_loads(k, (2,))
        for b in range(2):
            h = jnp.dot(f_v[b], tok_v[k, b * BS : (b + 1) * BS, :], preferred_element_type=F32)
            h_send[k, :, :, b] = h.astype(BF16).reshape(SEQ, 2, G, cw)

    load_first.wait()
    make_h(0)
    pl.semaphore_wait(barrier, SEQ - 1 + DP - 1)
    send(h_send, h_recv, 0, h_ss, h_rs)
    start_loads(1, (0, 1))

    load_second.wait()
    n = G * NB
    spread = (iota((n, NB), 0) // G == iota((n, NB), 1)).astype(BF16)
    same = iota((n, n), 0) // NB == iota((n, n), 1) % G
    same_t = iota((n, n), 1) // NB == iota((n, n), 0) % G
    for g in range(2):
        wt = lax.dot_general(
            spread, s_v[g * n : (g + 1) * n, :], NT, preferred_element_type=F32
        )
        wt_v[g] = jnp.where(same_t, wt, 0.0).astype(BF16)

    def make_hg(k):
        wait_loads(k, (0, 1))
        for g in range(2):
            rows = slice(g * n, (g + 1) * n)
            m = (cot_v[k, rows, :].astype(F32) * mg_v[k, rows, :].astype(F32)).astype(BF16)
            mg_v[k, rows, :] = m
            hg = jnp.dot(wt_v[g], m, preferred_element_type=F32).astype(BF16)
            hg_send[k, :, :, g] = hg.reshape(SEQ, 2, G, cw)

    start_loads(2, (0, 1))

    def load_pair(k):
        @pl.when(k < CHUNKS - 3)
        def _():
            start_loads(k + 3, (0, 1))

    def hg_first(k, carry):
        load_pair(k)
        make_hg(k)
        send(hg_send, hg_recv, k, hg_ss, hg_rs)
        return carry

    def hg_rest(k, carry):
        load_pair(k)
        make_hg(k)
        return carry

    lax.fori_loop(0, WINDOW - 1, hg_first, 0)
    lax.fori_loop(WINDOW - 1, CHUNKS, hg_rest, 0)

    def start_item(n):
        @pl.when(n <= CHUNKS)
        def _():
            send(hg_send, hg_recv, n - 1, hg_ss, hg_rs)

        @pl.when((n > CHUNKS) & (n < 2 * CHUNKS))
        def _():
            send(h_send, h_recv, n - CHUNKS, h_ss, h_rs)

    def wait_item(n):
        @pl.when((n > 0) & (n <= CHUNKS))
        def _():
            wait_sent(hg_send, n - 1, hg_ss)

        @pl.when(n > CHUNKS)
        def _():
            wait_sent(h_send, n - CHUNKS, h_ss)

        @pl.when(n == 0)
        def _():
            wait_sent(h_send, 0, h_ss)

    def next_item(n):
        wait_item(n)
        start_item(n + WINDOW)

    def load_tok(k, carry):
        start_loads(k, (2,))
        return carry

    lax.fori_loop(1, CHUNKS, load_tok, 0)
    for g in range(2):
        w = lax.dot_general(
            s_v[g * n : (g + 1) * n, :], spread, NT, preferred_element_type=F32
        )
        w_v[g] = jnp.where(same, w, 0.0).astype(BF16)

    def h_step(k, carry):
        make_h(k)
        return carry

    lax.fori_loop(1, CHUNKS, h_step, 0)
    for b in range(2):
        ft_v[b] = f_v[b].T

    facc[...] = jnp.zeros_like(facc)
    sacc[...] = jnp.zeros_like(sacc)

    def back_step(k, carry):
        next_item(k)
        wait_all(hg_recv, k, hg_rs)
        cols = pl.ds(pl.multiple_of(k * cw, cw), cw)
        for b in range(2):
            hg = hg_recv[k, :, b].reshape(BS, cw)
            rows = slice(b * BS, (b + 1) * BS)
            ig[rows, cols] = jnp.dot(ft_v[b], hg, preferred_element_type=F32).astype(BF16)
            terms = lax.dot_general(hg, tok_v[k, rows, :], NT, preferred_element_type=F32)
            facc[b] += terms.reshape(4, 2, 64, BS)
        return carry

    lax.fori_loop(0, CHUNKS, back_step, 0)

    def z_copy(d):
        t = (z + d) % 4
        return pltpu.make_async_remote_copy(
            src_ref=facc.at[:, t], dst_ref=zrecv.at[d - 1],
            send_sem=z_ss.at[d - 1], recv_sem=z_rs.at[d - 1],
            device_id=(t * 2 + xl, me), device_id_type=MESH,
        )

    x_copy = pltpu.make_async_remote_copy(
        src_ref=xsend, dst_ref=xrecv, send_sem=x_ss, recv_sem=x_rs,
        device_id=(z * 2 + 1 - xl, me), device_id_type=MESH,
    )
    for d in (1, 2, 3):
        z_copy(d).start()

    def second_terms(k):
        for g in range(2):
            h = h_recv[k, :, g].reshape(n, cw)
            m = mg_v[k, g * n : (g + 1) * n, :]
            terms = lax.dot_general(m, h, NT, preferred_element_type=F32)
            terms = jnp.where(same, terms, 0.0).reshape(G, NB, n)
            sacc[g] += jnp.sum(terms, axis=0)

    def gate_part(k):
        cols = pl.ds(pl.multiple_of(k * cw, cw), cw)
        for g in range(2):
            h = h_recv[k, :, g].reshape(n, cw)
            rows = slice(g * n, (g + 1) * n)
            mixed = jnp.dot(w_v[g], h, preferred_element_type=F32)
            gg[rows, cols] = (cot_v[k, rows, :].astype(F32) * mixed).astype(BF16)

    order = ((2, 1), (1, 1), (3, 1), (2, 0), (1, 0), (3, 0), (0, 1))

    def s_copy(p):
        dz, dx = order[p]
        t = (z + dz) % 4 * 2 + (xl + dx) % 2
        return pltpu.make_async_remote_copy(
            src_ref=sec_send.at[t], dst_ref=sec_recv.at[p],
            send_sem=s_ss.at[p], recv_sem=s_rs.at[p],
            device_id=(t, me), device_id_type=MESH,
        )

    def sum_z():
        for d in (1, 2, 3):
            z_copy(d).wait()
        for b in range(2):
            other = facc[b, z, 1 - xl] + zrecv[0, b, 1 - xl] + zrecv[1, b, 1 - xl] + zrecv[2, b, 1 - xl]
            xsend[b] = other.astype(BF16)
        x_copy.start()
        for b in range(2):
            xkeep[b] = facc[b, z, xl] + zrecv[0, b, xl] + zrecv[1, b, xl] + zrecv[2, b, xl]

    def share_second():
        for d in range(DP):
            part = jnp.concatenate([sacc[0, 4 * d : 4 * d + 4], sacc[1, 4 * d : 4 * d + 4]], axis=0)
            part = jnp.concatenate([part[:, : n // 2], part[:, n // 2 :]], axis=0)
            sec_own[d] = part
            sec_send[d] = part.astype(BF16)
        for p in range(DP - 1):
            s_copy(p).start()

    def forth_step(k, carry):
        pl.when(k < CHUNKS - 1)(lambda: next_item(k + CHUNKS))
        wait_all(h_recv, k, h_rs)
        second_terms(k)
        pl.when(k == CHUNKS // 2)(sum_z)
        pl.when(k == CHUNKS - 1)(share_second)
        gate_part(k)
        return carry

    lax.fori_loop(0, CHUNKS, forth_step, 0)
    x_copy.wait()
    fo[...] = (xkeep[...] + xrecv[...].astype(F32)) * scale

    wait_item(2 * CHUNKS - 1)
    total = sec_own[dp]
    for p in reversed(range(DP - 1)):
        s_copy(p).wait()
        total = total + sec_recv[p].astype(F32)
    so[:, : n // 2] = total[:8] * scale
    so[:, n // 2 :] = total[8:] * scale


def write_out(ig, gg, fo, so, ig_out, gg_out, fo_out, so_out, so_v, sem):
    rows = ig.shape[0] // 2
    copies = [pltpu.make_async_copy(fo, fo_out, sem.at[4])]
    for a in range(2):
        part = pl.ds(a * rows, rows)
        copies.append(pltpu.make_async_copy(ig.at[part], ig_out.at[part], sem.at[a]))
        copies.append(pltpu.make_async_copy(gg.at[part], gg_out.at[part], sem.at[2 + a]))
    for copy in copies:
        copy.start()
    n = G * NB
    gather = (iota((n, NB), 0) // G == iota((n, NB), 1)).astype(F32)
    own = iota((G, 4, n), 0) == iota((G, 4, n), 2) % G
    for g in range(2):
        wide = jnp.where(own, so[4 * g : 4 * g + 4][None], 0.0).reshape(G * 4, n)
        share = jnp.dot(
            wide, gather, precision=lax.Precision.HIGHEST, preferred_element_type=F32
        )
        for i in range(G):
            so_v[g * G + i] = share[4 * i : 4 * i + 4]
    copies.append(pltpu.make_async_copy(so_v, so_out, sem.at[5]))
    copies[-1].start()
    for copy in copies:
        copy.wait()


def local(tokens, gate, cotangent, first_factor, second_factor):
    seqs, rows, width = tokens.shape
    scale = 1.0 / math.sqrt(width * seqs * DP)
    cw = width // CHUNKS
    flat = (rows, width)
    vm = pltpu.VMEM
    dma = pltpu.SemaphoreType.DMA
    out = (
        vm(flat, BF16), vm(flat, BF16), vm((2, 64, BS), F32), vm((8, G * NB), F32),
    )
    scratch = [
        vm((CHUNKS, rows, cw), BF16), vm((CHUNKS, rows, cw), BF16), vm((CHUNKS, rows, cw), BF16),
        vm((2, BS, BS), BF16), vm((2, BS, BS), BF16), vm((BS * 2, NB), BF16),
        vm((2, BS, BS), BF16), vm((2, BS, BS), BF16),
        vm((CHUNKS, SEQ, 2, 2, G, cw), BF16), vm((CHUNKS, SEQ, 2, 2, G, cw), BF16),
        vm((CHUNKS, SEQ, 2, 2, G, cw), BF16), vm((CHUNKS, SEQ, 2, 2, G, cw), BF16),
        vm((2, 4, 2, 64, BS), F32), vm((2, NB, G * NB), F32), vm((3, 2, 2, 64, BS), F32),
        vm((2, 64, BS), BF16), vm((2, 64, BS), BF16), vm((2, 64, BS), F32),
        vm((DP, 16, G * NB // 2), F32), vm((DP, 16, G * NB // 2), BF16), vm((DP - 1, 16, G * NB // 2), BF16),
        dma((3, CHUNKS)), dma((2,)),
        dma((CHUNKS,)), dma((CHUNKS,)), dma((CHUNKS,)), dma((CHUNKS,)),
        dma((3,)), dma((3,)), dma, dma, dma((DP - 1,)), dma((DP - 1,)),
    ]
    hbm = pl.BlockSpec(memory_space=pl.ANY)
    inner = pl.BlockSpec(memory_space=pltpu.VMEM)
    ig, gg, fo, so = pl.pallas_call(
        functools.partial(kernel, width, scale),
        out_shape=out,
        in_specs=[hbm] * 5,
        out_specs=[inner] * 4,
        scratch_shapes=scratch,
        compiler_params=pltpu.CompilerParams(
            collective_id=0, has_side_effects=True, vmem_limit_bytes=52 * 2**20
        ),
        cost_estimate=pl.CostEstimate(
            flops=15 * 2**30, bytes_accessed=22 * 2**20, transcendentals=0
        ),
        name="mixer",
    )(
        tokens.reshape(flat), gate.reshape(flat), cotangent.reshape(flat),
        first_factor, second_factor.reshape(BS * 2, NB),
    )
    ig, gg, fo, so = pl.pallas_call(
        write_out,
        out_shape=(
            jax.ShapeDtypeStruct(flat, BF16), jax.ShapeDtypeStruct(flat, BF16),
            jax.ShapeDtypeStruct((2, 64, BS), F32), jax.ShapeDtypeStruct((NB, 4, NB), F32),
        ),
        in_specs=[inner] * 4,
        out_specs=[hbm] * 4,
        scratch_shapes=[vm((NB, 4, NB), F32), dma((6,))],
        compiler_params=pltpu.CompilerParams(vmem_limit_bytes=8 * 2**20),
        name="write_out",
    )(ig, gg, fo, so)
    return (ig.reshape(seqs, rows, width), gg.reshape(seqs, rows, width), fo, so)


def solution(mesh):
    placed = (
        P("dp", "seq", None),
        P("dp", "seq", None),
        P("dp", "seq", None),
        P("seq", None, None),
        P("seq", None, None),
    )
    return jax.shard_map(
        local,
        mesh=mesh,
        in_specs=placed,
        out_specs=(
            P("dp", "seq", None),
            P("dp", "seq", None),
            P("seq", "dp", None),
            P("seq", "dp", None),
        ),
        check_vma=False,
    )
```
